512 devices in a mesh: ctx: 32 (over z, core), head: 16 (over y, x).
Axes of the slice: x: 4, y: 4, z: 16, core: 2. Of those that a mesh axis runs over, the one named last changes fastest.
Arguments:
- tokens: bfloat16 [16384, 4096], P('ctx', 'head'), may hold values from -8 to 8
- norm_gain: bfloat16 [4096], P('head'), may hold values from 0.099609375 to 1.8984375
- w_qkv: bfloat16 [3, 4096, 2048], P(None, None, 'head'), may hold values from -2 to 2
- doc_lengths: int32 [2], replicated, may hold values from 1 to 15360, 16384 in all
- span_start: int32 [8], replicated, may hold values from 0 to 16383, as said below
- span_len: int32 [8], replicated, may hold values from 256 to 1024, as said below
Outputs:
- attended: bfloat16 [16384, 2048], P('ctx', 'head')
The draws below stay inside these ranges and needn't reach their ends.
Inputs may be any that keep to these rules, and one draw needn't show every extreme that they name: `span_start`: image k lies inside positions k * 2048 to (k + 1) * 2048 - 1; images don't intersect. `span_len`: one image has exactly 1024 tokens. `doc_lengths`: the lengths sum to 16384.
All inputs are finite; a program needn't handle non-finite values.
Results may differ from the reference program's by a relative error of at most 0.012.
The reference program's roundings to bfloat16 on the way (of `normed` and `weights`) count: a program that leaves them out, or rounds other values in their place, can miss the bound.
Values may be sent and summed in bfloat16 or wider, within the bound.
No kernel may reach another device: no remote copies, remote signals or barrier semaphores. Data moves between devices by JAX's collectives and lax.ppermute only.
A program may use at most 64 MiB of HBM per device.

```python
import math
import jax
import jax.numpy as jnp
import numpy as np
from jax import lax

D = 4096
HD = 128
TOK_DEV = 512
HEADS = 16
LENGTH = 16384
IMG_MAX = 1024
SPANS = 8
DOCS = 2


def spans_common(key):
    slot = LENGTH // SPANS
    lengths = jax.random.randint(jax.random.fold_in(key, 101), (SPANS,), IMG_MAX // 4, IMG_MAX + 1)
    picked = jax.random.randint(jax.random.fold_in(key, 102), (), 0, SPANS)
    lengths = jnp.where(jnp.arange(SPANS) == picked, IMG_MAX, lengths).astype(jnp.int32)
    raw = jax.random.randint(jax.random.fold_in(key, 103), (SPANS,), 0, 1048576)
    offsets = raw % (slot - lengths + 1)
    starts = (jnp.arange(SPANS) * slot + offsets).astype(jnp.int32)
    return (starts, lengths)


def draw_tokens(key, part):
    key = jax.random.fold_in(key, 11)
    return jnp.clip(jax.random.normal(key, (LENGTH, D), jnp.float32), -6.0, 6.0).astype(jnp.bfloat16)


def draw_w_qkv(key, part):
    key = jax.random.fold_in(key, 12)
    sharpen = jnp.array([1.7, 1.7, 1.0], jnp.float32)
    matrix = jnp.clip(jax.random.normal(key, (3, D, HEADS * HD), jnp.float32), -6.0, 6.0) * D ** (-0.5) * sharpen[:, None, None]
    return matrix.astype(jnp.bfloat16)


def draw_span_start(key, part):
    starts, lengths = spans_common(key)
    return starts


def draw_span_len(key, part):
    starts, lengths = spans_common(key)
    return lengths


def length_profile(count, total, limit, skew):
    weights = [(1 << 20) // math.isqrt(rank ** skew) + 1 for rank in range(2, count + 1)]
    rest, given = total - limit - (count - 1), [1] * (count - 1)
    while rest > 0:
        free = [i for i in range(count - 1) if given[i] < limit]
        whole, left = sum([weights[i] for i in free]), rest
        for i in free:
            more = min(limit - given[i], max(1, left * weights[i] // whole), rest)
            given[i] = given[i] + more
            rest = rest - more
    return np.array([limit] + given)


def ragged_sizes(key, count, total, most, skew):
    if count == 2:
        one = jax.random.randint(key, (), max(1, total - most), min(most, total - 1) + 1)
        return jnp.stack([one, total - one])
    tallies = jnp.asarray(length_profile(count, total, most, skew), jnp.int32)
    pairs = (count - 1) // 2
    giver, sink = tallies[1:1 + 2 * pairs:2], tallies[2:2 + 2 * pairs:2]
    slack = jnp.minimum(giver - 1, most - sink)
    moved = jax.random.randint(jax.random.fold_in(key, 1), (pairs,), 0, 1 << 20) % (slack + 1)
    tallies = tallies.at[1:1 + 2 * pairs:2].set(giver - moved).at[2:2 + 2 * pairs:2].set(sink + moved)
    return tallies[jax.random.permutation(jax.random.fold_in(key, 2), count)]


def setup_inputs(seed: int = 0) -> dict:
    seeds = jax.random.split(jax.random.key(seed), 7)
    return {
        "tokens": draw_tokens(jax.random.fold_in(seeds[6], 71), 0),
        "norm_gain": jnp.clip(1.0 + 0.18 * jax.random.normal(seeds[1], (D,), jnp.float32), 0.099609375, 1.8984375).astype(jnp.bfloat16),
        "w_qkv": draw_w_qkv(jax.random.fold_in(seeds[6], 71), 0),
        "doc_lengths": ragged_sizes(seeds[3], DOCS, LENGTH, LENGTH - (DOCS - 1) * (LENGTH // 16), 2).astype(jnp.int32),
        "span_start": draw_span_start(jax.random.fold_in(seeds[6], 71), 0),
        "span_len": draw_span_len(jax.random.fold_in(seeds[6], 71), 0),
    }


EPS = 1e-05
NEG = -1e+30

def row_meta(idx, doc_lengths, span_start, span_len):
    starts = jnp.cumsum(doc_lengths) - doc_lengths
    after = (idx[:, None] >= starts[None, :]).astype(jnp.int32)
    doc = lax.optimization_barrier(jnp.sum(after, axis=1)) - 1
    ranks = jnp.arange(doc_lengths.shape[0], dtype=jnp.int32)
    doc_start = lax.optimization_barrier(jnp.sum(jnp.where(doc[:, None] == ranks[None, :], starts[None, :], 0), axis=1))
    ends = span_start + span_len
    inside = (idx[:, None] >= span_start[None, :]) & (idx[:, None] < ends[None, :])
    images = jnp.arange(span_start.shape[0], dtype=jnp.int32)
    image = lax.optimization_barrier(jnp.sum(jnp.where(inside, images[None, :] + 1, 0), axis=1)) - 1
    reach = jnp.maximum(idx, lax.optimization_barrier(jnp.max(jnp.where(inside, ends[None, :] - 1, 0), axis=1)))
    return (doc, doc_start, image, reach)

def rotate(values, pos):
    half = values.shape[-1] // 2
    freqs = jnp.power(jnp.float32(500000.0), -2.0 * jnp.arange(half, dtype=jnp.float32) / values.shape[-1])
    angle = pos.astype(jnp.float32)[:, None] * freqs[None, :]
    cosine = jnp.cos(angle)
    sine = jnp.sin(angle)
    first = values[:, :half]
    second = values[:, half:]
    return jnp.concatenate([first * cosine - second * sine, second * cosine + first * sine], axis=1)

def reference(tokens, norm_gain, w_qkv, doc_lengths, span_start, span_len):
    tokf = tokens.astype(jnp.float32)
    scale = lax.rsqrt(lax.optimization_barrier(jnp.mean(tokf * tokf, axis=1, keepdims=True)) + EPS)
    normed = (tokf * scale * norm_gain.astype(jnp.float32)).astype(jnp.bfloat16)
    normf = normed.astype(jnp.float32)
    heads = w_qkv.shape[2] // HD
    idx = jnp.arange(LENGTH, dtype=jnp.int32)
    doc, doc_start, image, reach = row_meta(idx, doc_lengths, span_start, span_len)
    pos = idx - doc_start

    def one_head(head_index):
        w_head = lax.dynamic_slice_in_dim(w_qkv, head_index * HD, HD, 2).astype(jnp.float32)
        qkv = jnp.einsum('td,sdh->sth', normf, w_head)
        query = rotate(qkv[0], pos).astype(jnp.bfloat16)
        keys = rotate(qkv[1], pos).astype(jnp.bfloat16)
        values = qkv[2].astype(jnp.bfloat16)

        def block(block_index):
            first = block_index * TOK_DEV
            q_rows = lax.dynamic_slice_in_dim(query, first, TOK_DEV, 0)
            q_idx = first + jnp.arange(TOK_DEV, dtype=jnp.int32)
            q_doc = lax.dynamic_slice_in_dim(doc, first, TOK_DEV, 0)
            q_img = lax.dynamic_slice_in_dim(image, first, TOK_DEV, 0)
            scores = jnp.dot(q_rows, keys.T, preferred_element_type=jnp.float32) * HD ** (-0.5)
            allowed = (q_doc[:, None] == doc[None, :]) & ((idx[None, :] <= q_idx[:, None]) | (q_img[:, None] == image[None, :]) & (q_img[:, None] >= 0))
            top = lax.optimization_barrier(jnp.max(jnp.where(allowed, scores, NEG), axis=1, keepdims=True))
            weights = jnp.where(allowed, jnp.exp(scores - top), 0.0)
            total = lax.optimization_barrier(jnp.sum(weights, axis=1, keepdims=True))
            summed = jnp.dot(weights.astype(jnp.bfloat16), values, preferred_element_type=jnp.float32)
            return (summed / total).astype(jnp.bfloat16)
        blocks = lax.map(block, jnp.arange(LENGTH // TOK_DEV, dtype=jnp.int32))
        return blocks.reshape(LENGTH, HD)
    outs = lax.map(one_head, jnp.arange(heads, dtype=jnp.int32))
    return jnp.transpose(outs, (1, 0, 2)).reshape(LENGTH, heads * HD)
```

```python
import functools
import math

import jax
import jax.numpy as jnp
from jax import lax
from jax.experimental import pallas as pl
from jax.experimental.pallas import tpu as pltpu
from jax.sharding import Mesh, PartitionSpec as P

D = 4096
HD = 128
EPS = 1e-05
NEG = -1e30
ROWS = 512
FEAT = 256
PAD = 16
NZ = 16
C2 = math.log2(math.e) * HD**-0.5
STEPS = (0, 1, -1, 2)


def row_meta(idx, doc_lengths, span_start, span_len):
    starts = jnp.cumsum(doc_lengths) - doc_lengths
    mine = (idx[:, None] >= starts[None, :]) & (idx[:, None] < (starts + doc_lengths)[None, :])
    first = jnp.sum(jnp.where(mine, starts[None, :], 0), axis=1)
    last = jnp.sum(jnp.where(mine, (starts + doc_lengths)[None, :], 0), axis=1) - 1
    ends = span_start + span_len
    inside = (idx[:, None] >= span_start[None, :]) & (idx[:, None] < ends[None, :])
    reach = jnp.maximum(idx, jnp.max(jnp.where(inside, ends[None, :] - 1, 0), axis=1))
    return first, jnp.minimum(reach, last)


def angles(pos):
    half = HD // 2
    freqs = jnp.power(jnp.float32(500000.0), -2.0 * jnp.arange(half, dtype=jnp.float32) / HD)
    angle = pos.astype(jnp.float32)[:, None] * freqs[None, :]
    cosine = jnp.cos(angle)
    sine = jnp.sin(angle)
    return (
        jnp.concatenate([cosine, cosine], axis=1),
        jnp.concatenate([-sine, sine], axis=1),
    )


def qkv_kernel(blk_ref, *refs):
    sets, (w_ref, cos_ref, sin_ref, q_ref, kv_ref, nrm) = refs[:8], refs[8:]
    tile = 64

    def norm_rows(i, carry):
        r = pl.multiple_of(i * tile, tile)
        acc = jnp.zeros((tile, FEAT), jnp.float32)
        for b in range(16):
            x = sets[b // 2][b % 2, pl.ds(r, tile), :].astype(jnp.float32)
            acc = acc + x * x
        scale = lax.rsqrt(jnp.sum(acc, axis=1, keepdims=True) / D + EPS)
        for b in range(16):
            x = sets[b // 2][b % 2, pl.ds(r, tile), :].astype(jnp.float32)
            gain = sets[b // 2][b % 2, ROWS : ROWS + 1, :].astype(jnp.float32)
            col = pl.multiple_of(blk_ref[b] * FEAT, FEAT)
            nrm[pl.ds(r, tile), pl.ds(col, FEAT)] = (x * scale * gain).astype(jnp.bfloat16)
        return carry

    lax.fori_loop(0, ROWS // tile, norm_rows, 0)
    out = jnp.dot(nrm[...], w_ref[...], preferred_element_type=jnp.float32)
    cosine, sine = cos_ref[...], sin_ref[...]

    def rotate(v):
        return (v * cosine + pltpu.roll(v, HD // 2, 1) * sine).astype(jnp.bfloat16)

    q_ref[...] = rotate(out[:, :HD])
    kv_ref[:ROWS, :] = rotate(out[:, HD : 2 * HD])
    vt = out[:, 2 * HD :].T.astype(jnp.bfloat16)
    for b in range(ROWS // HD):
        kv_ref[ROWS + b * HD : ROWS + (b + 1) * HD, :] = vt[:, b * HD : (b + 1) * HD]


def project(blk, sets, w, cosine, sine):
    vmem = pl.BlockSpec(memory_space=pltpu.VMEM)
    return pl.pallas_call(
        qkv_kernel,
        out_shape=(
            jax.ShapeDtypeStruct((ROWS, HD), jnp.bfloat16),
            jax.ShapeDtypeStruct((2 * ROWS, HD), jnp.bfloat16),
        ),
        in_specs=[pl.BlockSpec(memory_space=pltpu.SMEM)] + [vmem] * 11,
        out_specs=(vmem, vmem),
        scratch_shapes=[pltpu.VMEM((ROWS, D), jnp.bfloat16)],
        compiler_params=pltpu.CompilerParams(vmem_limit_bytes=40 * 2**20),
        cost_estimate=pl.CostEstimate(
            flops=2 * ROWS * D * 3 * HD, bytes_accessed=8 * 2**20, transcendentals=0
        ),
        name="norm_qkv",
    )(blk, *sets, w, cosine, sine)


def attend_kernel(offs, fresh, meta_ref, q_ref, lo_ref, hi_ref, *refs):
    n = len(offs)
    kvs, st = refs[:n], refs[-1]
    if fresh:
        row = lax.broadcasted_iota(jnp.int32, st.shape, 1)
        st[...] = jnp.where(row == HD, NEG, 0.0)
    else:
        st[...] = refs[n][...]
    wide = 256
    per = ROWS // wide
    firsts = [
        (lax.rem(meta_ref[8] + (off + NZ), NZ) * 2 + meta_ref[9]) * ROWS for off in offs
    ]

    def part(js, masked, i, carry):
        t = i // per
        cols = pl.ds(pl.multiple_of((i % per) * wide, wide), wide)
        query = q_ref[t, cols, :]
        ss = [
            lax.dot_general(
                kvs[j][:ROWS, :], query, (((1,), (1,)), ((), ())), preferred_element_type=jnp.float32
            )
            for j in js
        ]
        oks = [None] * len(js)
        if masked:
            lo, hi = lo_ref[t, :, cols], hi_ref[t, :, cols]
            row = lax.broadcasted_iota(jnp.int32, ss[0].shape, 0)
            oks = [(row >= lo - firsts[j]) & (row <= hi - firsts[j]) for j in js]
            ss = [jnp.where(ok, s, NEG) for ok, s in zip(oks, ss)]
        m_old = st[t, HD : HD + 1, cols]
        m_new = m_old
        for s in ss:
            m_new = jnp.maximum(m_new, jnp.max(s, axis=0, keepdims=True))
        alpha = jnp.exp2((m_old - m_new) * C2)
        total = st[t, HD + 1 : HD + 2, cols] * alpha
        acc = st[t, :HD, cols] * alpha
        shift = m_new * C2
        for j, s, ok in zip(js, ss, oks):
            p = jnp.exp2(s * C2 - shift)
            if masked:
                p = jnp.where(ok, p, 0.0)
            total = total + jnp.sum(p, axis=0, keepdims=True)
            vt = jnp.concatenate(
                [kvs[j][ROWS + b * HD : ROWS + (b + 1) * HD, :] for b in range(ROWS // HD)], axis=1
            )
            acc = acc + jnp.dot(vt, p.astype(jnp.bfloat16), preferred_element_type=jnp.float32)
        st[t, HD : HD + 1, cols] = m_new
        st[t, HD + 1 : HD + 2, cols] = total
        st[t, :HD, cols] = acc
        return carry

    needed, whole = {}, []
    for j in range(n):
        last = firsts[j] + ROWS - 1
        for t in range(2):
            needed[j, t] = (firsts[j] <= meta_ref[4 * t + 3]) & (last >= meta_ref[4 * t])
            whole.append((firsts[j] >= meta_ref[4 * t + 1]) & (last <= meta_ref[4 * t + 2]))
    every = functools.reduce(jnp.logical_and, whole)

    @pl.when(every)
    def _():
        lax.fori_loop(0, 2 * per, functools.partial(part, range(n), False), 0)

    for j in range(n):

        @pl.when(jnp.logical_not(every) & (needed[j, 0] | needed[j, 1]))
        def _(j=j):
            begin = jnp.where(needed[j, 0], 0, per)
            end = jnp.where(needed[j, 1], 2 * per, per)
            lax.fori_loop(begin, end, functools.partial(part, [j], True), 0)


def attend(meta, q, lo, hi, kvs, offs, state):
    n = len(kvs)
    vmem = pl.BlockSpec(memory_space=pltpu.VMEM)
    state = [] if state is None else [state]
    pairs = 2 * ROWS * ROWS * n
    return pl.pallas_call(
        functools.partial(attend_kernel, offs, not state),
        out_shape=jax.ShapeDtypeStruct((2, HD + 8, ROWS), jnp.float32),
        in_specs=[pl.BlockSpec(memory_space=pltpu.SMEM)] + [vmem] * (3 + n + len(state)),
        out_specs=vmem,
        input_output_aliases={4 + n: 0} if state else {},
        compiler_params=pltpu.CompilerParams(vmem_limit_bytes=40 * 2**20),
        cost_estimate=pl.CostEstimate(
            flops=4 * pairs * HD, bytes_accessed=2 * 2**20, transcendentals=pairs
        ),
        name="attend",
    )(meta, q, lo, hi, *kvs, *state)


def merge_kernel(a_ref, b_ref, o_ref):
    ma, mb = a_ref[HD : HD + 1, :], b_ref[HD : HD + 1, :]
    m = jnp.maximum(ma, mb)
    wa, wb = jnp.exp2((ma - m) * C2), jnp.exp2((mb - m) * C2)
    total = a_ref[HD + 1 : HD + 2, :] * wa + b_ref[HD + 1 : HD + 2, :] * wb
    out = (a_ref[:HD, :] * wa + b_ref[:HD, :] * wb) / total
    o_ref[...] = out.T.astype(jnp.bfloat16)


def merge(a, b):
    return pl.pallas_call(
        merge_kernel, out_shape=jax.ShapeDtypeStruct((ROWS, HD), jnp.bfloat16), name="merge"
    )(a, b)


def plane_perm(d, first):
    out = []
    for c in range(2):
        for y in range(4):
            for x in range(4):
                if (c == 0) == first:
                    to = (y, (x + d) % 4)
                else:
                    to = ((y + d) % 4, x)
                out.append(((c * 4 + y) * 4 + x, (c * 4 + to[0]) * 4 + to[1]))
    return out


def ring(n, d):
    return [(i, (i + d) % n) for i in range(n)]


def body(tokens, norm_gain, w_qkv, doc_lengths, span_start, span_len):
    z, core = lax.axis_index("z"), lax.axis_index("core")
    y, x = lax.axis_index("y"), lax.axis_index("x")
    plane = ("core", "y", "x")

    mine = jnp.concatenate([tokens, jnp.broadcast_to(norm_gain[None, :], (PAD, FEAT))], axis=0)
    side = {d: lax.ppermute(mine, plane, plane_perm(d, True)) for d in (1, -1, 2)}
    a, b = jnp.stack([mine, side[1]]), jnp.stack([side[-1], side[2]])
    far = lambda v, d: lax.ppermute(v, plane, plane_perm(d, False))
    left_a, right_b = far(a, 1), far(b, -1)
    left_b, right_a = far(b, 1), far(a, -1)
    sets = [a, b, left_a, left_b, right_a, right_b, far(left_a, 1), far(right_b, -1)]
    dk = jnp.array([k for k in STEPS for j in STEPS], jnp.int32)
    dj = jnp.array([j for k in STEPS for j in STEPS], jnp.int32)
    on_x = jnp.where(core == 0, dj, dk)
    on_y = jnp.where(core == 0, dk, dj)
    blk = ((y - on_y + 4) % 4) * 4 + (x - on_x + 4) % 4

    offs = jnp.arange(ROWS, dtype=jnp.int32)
    first_of = lambda c: (z * 2 + c) * ROWS
    lows, highs = [], []
    for c in (core, 1 - core):
        low, high = row_meta(first_of(c) + offs, doc_lengths, span_start, span_len)
        lows.append(low)
        highs.append(high)
    cosine, sine = angles(first_of(core) + offs - lows[0])
    lo, hi = jnp.stack(lows)[:, None, :], jnp.stack(highs)[:, None, :]
    slot = jnp.arange(16, dtype=jnp.int32)
    at = first_of(jnp.where(slot < 4, core, 1 - core)) + (slot % 2) * (ROWS - 1)
    low, high = row_meta(at, doc_lengths, span_start, span_len)
    meta = jnp.where(slot % 4 < 2, low, high)
    meta = jnp.where(slot == 8, z, jnp.where(slot == 9, core, meta)).astype(jnp.int32)

    w = jnp.concatenate([w_qkv[0], w_qkv[1], w_qkv[2]], axis=1)
    q, kv = project(blk, sets, w, cosine, sine)

    up = down = kv
    q2 = jnp.stack([q, lax.ppermute(q, "core", ring(2, 1))], axis=0)
    state = None
    arrived, sources = [kv], [0]
    for i in range(1, NZ // 2 + 1):
        up = lax.ppermute(up, "z", ring(NZ, 1))
        new, src = [up], [-i]
        if i < NZ // 2:
            down = lax.ppermute(down, "z", ring(NZ, -1))
            new, src = new + [down], src + [i]
        state = attend(meta, q2, lo, hi, arrived, sources, state)
        up, state = lax.optimization_barrier((up, state))
        new[0] = up
        arrived, sources = new, src
    state = attend(meta, q2, lo, hi, arrived, sources, state)
    other = lax.ppermute(state[1], "core", ring(2, 1))
    return merge(state[0], other)


def solution(mesh):
    fine = Mesh(mesh.devices.reshape(NZ, 2, 4, 4), ("z", "core", "y", "x"))
    both, plane = ("z", "core"), ("y", "x")
    return jax.shard_map(
        body,
        mesh=fine,
        in_specs=(P(both, plane), P(plane), P(None, None, plane), P(), P(), P()),
        out_specs=P(both, plane),
        check_vma=False,
    )
```

```python
import functools
import math

import jax
import jax.numpy as jnp
from jax import lax
from jax.experimental import pallas as pl
from jax.experimental.pallas import tpu as pltpu
from jax.sharding import Mesh, PartitionSpec as P

D = 4096
HD = 128
EPS = 1e-05
NEG = -1e30
ROWS = 512
FEAT = 256
PAD = 16
NZ = 16
C2 = math.log2(math.e) * HD**-0.5
STEPS = (0, 1, -1, 2)


def row_meta(idx, doc_lengths, span_start, span_len):
    starts = jnp.cumsum(doc_lengths) - doc_lengths
    mine = (idx[:, None] >= starts[None, :]) & (idx[:, None] < (starts + doc_lengths)[None, :])
    first = jnp.sum(jnp.where(mine, starts[None, :], 0), axis=1)
    last = jnp.sum(jnp.where(mine, (starts + doc_lengths)[None, :], 0), axis=1) - 1
    ends = span_start + span_len
    inside = (idx[:, None] >= span_start[None, :]) & (idx[:, None] < ends[None, :])
    reach = jnp.maximum(idx, jnp.max(jnp.where(inside, ends[None, :] - 1, 0), axis=1))
    return first, jnp.minimum(reach, last)


def angles(pos):
    half = HD // 2
    freqs = jnp.power(jnp.float32(500000.0), -2.0 * jnp.arange(half, dtype=jnp.float32) / HD)
    angle = pos.astype(jnp.float32)[:, None] * freqs[None, :]
    cosine = jnp.cos(angle)
    sine = jnp.sin(angle)
    return (
        jnp.concatenate([cosine, cosine], axis=1),
        jnp.concatenate([-sine, sine], axis=1),
    )


def qkv_kernel(blk_ref, *refs):
    sets, (w_ref, cos_ref, sin_ref, q_ref, kv_ref, nrm) = refs[:8], refs[8:]
    tile = 64

    def norm_rows(i, carry):
        r = pl.multiple_of(i * tile, tile)
        acc = jnp.zeros((tile, FEAT), jnp.float32)
        for b in range(16):
            x = sets[b // 2][b % 2, pl.ds(r, tile), :].astype(jnp.float32)
            acc = acc + x * x
        scale = lax.rsqrt(jnp.sum(acc, axis=1, keepdims=True) / D + EPS)
        for b in range(16):
            x = sets[b // 2][b % 2, pl.ds(r, tile), :].astype(jnp.float32)
            gain = sets[b // 2][b % 2, ROWS : ROWS + 1, :].astype(jnp.float32)
            col = pl.multiple_of(blk_ref[b] * FEAT, FEAT)
            nrm[pl.ds(r, tile), pl.ds(col, FEAT)] = (x * scale * gain).astype(jnp.bfloat16)
        return carry

    lax.fori_loop(0, ROWS // tile, norm_rows, 0)
    out = jnp.dot(nrm[...], w_ref[...], preferred_element_type=jnp.float32)
    cosine, sine = cos_ref[...], sin_ref[...]

    def rotate(v):
        return (v * cosine + pltpu.roll(v, HD // 2, 1) * sine).astype(jnp.bfloat16)

    q_ref[...] = rotate(out[:, :HD])
    kv_ref[:ROWS, :] = rotate(out[:, HD : 2 * HD])
    vt = out[:, 2 * HD :].T.astype(jnp.bfloat16)
    for b in range(ROWS // HD):
        kv_ref[ROWS + b * HD : ROWS + (b + 1) * HD, :] = vt[:, b * HD : (b + 1) * HD]


def project(blk, sets, w, cosine, sine):
    vmem = pl.BlockSpec(memory_space=pltpu.VMEM)
    return pl.pallas_call(
        qkv_kernel,
        out_shape=(
            jax.ShapeDtypeStruct((ROWS, HD), jnp.bfloat16),
            jax.ShapeDtypeStruct((2 * ROWS, HD), jnp.bfloat16),
        ),
        in_specs=[pl.BlockSpec(memory_space=pltpu.SMEM)] + [vmem] * 11,
        out_specs=(vmem, vmem),
        scratch_shapes=[pltpu.VMEM((ROWS, D), jnp.bfloat16)],
        compiler_params=pltpu.CompilerParams(vmem_limit_bytes=40 * 2**20),
        cost_estimate=pl.CostEstimate(
            flops=2 * ROWS * D * 3 * HD, bytes_accessed=8 * 2**20, transcendentals=0
        ),
        name="norm_qkv",
    )(blk, *sets, w, cosine, sine)


def attend_kernel(offs, fresh, last_call, meta_ref, q_ref, lo_ref, hi_ref, *refs):
    n = len(offs)
    kvs, st = refs[:n], refs[-1]
    if fresh:
        row = lax.broadcasted_iota(jnp.int32, st.shape, 1)
        st[...] = jnp.where(row == HD, NEG, 0.0)
    else:
        st[...] = refs[n][...]
    wide = 512
    per = ROWS // wide
    z, core = meta_ref[8], meta_ref[9]
    firsts = [
        (lax.rem(z + off + NZ, NZ) * 2 + core) * ROWS for off in offs
    ]

    def part(js, masked, i, carry):
        t = i // per
        cols = pl.ds(pl.multiple_of((i % per) * wide, wide), wide)
        query = q_ref[t, cols, :]
        ss = [
            lax.dot_general(
                kvs[j][:ROWS, :], query, (((1,), (1,)), ((), ())), preferred_element_type=jnp.float32
            )
            for j in js
        ]
        oks = [None] * len(js)
        if masked:
            lo, hi = lo_ref[t, :, cols], hi_ref[t, :, cols]
            row = lax.broadcasted_iota(jnp.int32, ss[0].shape, 0)
            oks = [(row >= lo - firsts[j]) & (row <= hi - firsts[j]) for j in js]
            ss = [jnp.where(ok, s, NEG) for ok, s in zip(oks, ss)]
        m_old = st[t, HD : HD + 1, cols]
        m_new = m_old
        for s in ss:
            m_new = jnp.maximum(m_new, jnp.max(s, axis=0, keepdims=True))
        alpha = jnp.exp2((m_old - m_new) * C2)
        total = st[t, HD + 1 : HD + 2, cols] * alpha
        acc = st[t, :HD, cols] * alpha
        shift = m_new * C2
        for j, s, ok in zip(js, ss, oks):
            p = jnp.exp2(s * C2 - shift)
            if masked:
                p = jnp.where(ok, p, 0.0)
            total = total + jnp.sum(p, axis=0, keepdims=True)
            vt = jnp.concatenate(
                [kvs[j][ROWS + b * HD : ROWS + (b + 1) * HD, :] for b in range(ROWS // HD)], axis=1
            )
            acc = acc + jnp.dot(vt, p.astype(jnp.bfloat16), preferred_element_type=jnp.float32)
        st[t, HD : HD + 1, cols] = m_new
        st[t, HD + 1 : HD + 2, cols] = total
        st[t, :HD, cols] = acc
        return carry

    needed, whole = {}, []
    for j in range(n):
        last = firsts[j] + ROWS - 1
        for t in range(2):
            needed[j, t] = (firsts[j] <= meta_ref[4 * t + 3]) & (last >= meta_ref[4 * t])
            whole.append((firsts[j] >= meta_ref[4 * t + 1]) & (last <= meta_ref[4 * t + 2]))
    every = functools.reduce(jnp.logical_and, whole)

    @pl.when(every)
    def _():
        lax.fori_loop(0, 2 * per, functools.partial(part, range(n), False), 0)

    for j in range(n):

        @pl.when(jnp.logical_not(every) & (needed[j, 0] | needed[j, 1]))
        def _(j=j):
            begin = jnp.where(needed[j, 0], 0, per)
            end = jnp.where(needed[j, 1], 2 * per, per)
            lax.fori_loop(begin, end, functools.partial(part, [j], True), 0)


    if last_call:
        for t in range(2):
            refs[-3 + t][...] = st[t]


def attend(meta, q, lo, hi, kvs, offs, state, last_call=False):
    n = len(kvs)
    vmem = pl.BlockSpec(memory_space=pltpu.VMEM)
    state = [] if state is None else [state]
    pairs = 2 * ROWS * ROWS * n
    full = (2, HD + 8, ROWS)
    part = jax.ShapeDtypeStruct(full[1:], jnp.float32)
    return pl.pallas_call(
        functools.partial(attend_kernel, offs, not state, last_call),
        out_shape=(part, part) if last_call else jax.ShapeDtypeStruct(full, jnp.float32),
        in_specs=[pl.BlockSpec(memory_space=pltpu.SMEM)] + [vmem] * (3 + n + len(state)),
        out_specs=(vmem, vmem) if last_call else vmem,
        scratch_shapes=[pltpu.VMEM(full, jnp.float32)] if last_call else [],
        input_output_aliases={4 + n: 0} if state and not last_call else {},
        compiler_params=pltpu.CompilerParams(vmem_limit_bytes=40 * 2**20),
        cost_estimate=pl.CostEstimate(
            flops=4 * pairs * HD, bytes_accessed=2 * 2**20, transcendentals=pairs
        ),
        name="attend",
    )(meta, q, lo, hi, *kvs, *state)


def merge_kernel(a_ref, b_ref, o_ref):
    ma, mb = a_ref[HD : HD + 1, :], b_ref[HD : HD + 1, :]
    m = jnp.maximum(ma, mb)
    wa, wb = jnp.exp2((ma - m) * C2), jnp.exp2((mb - m) * C2)
    total = a_ref[HD + 1 : HD + 2, :] * wa + b_ref[HD + 1 : HD + 2, :] * wb
    out = (a_ref[:HD, :] * wa + b_ref[:HD, :] * wb) / total
    o_ref[...] = out.T.astype(jnp.bfloat16)


def merge(a, b):
    return pl.pallas_call(
        merge_kernel, out_shape=jax.ShapeDtypeStruct((ROWS, HD), jnp.bfloat16), name="merge"
    )(a, b)


def plane_perm(d, first):
    out = []
    for c in range(2):
        for y in range(4):
            for x in range(4):
                if (c == 0) == first:
                    to = (y, (x + d) % 4)
                else:
                    to = ((y + d) % 4, x)
                out.append(((c * 4 + y) * 4 + x, (c * 4 + to[0]) * 4 + to[1]))
    return out


def ring(n, d):
    return [(i, (i + d) % n) for i in range(n)]


def body(tokens, norm_gain, w_qkv, doc_lengths, span_start, span_len):
    z, core = lax.axis_index("z"), lax.axis_index("core")
    y, x = lax.axis_index("y"), lax.axis_index("x")
    plane = ("core", "y", "x")

    mine = jnp.concatenate([tokens, jnp.broadcast_to(norm_gain[None, :], (PAD, FEAT))], axis=0)
    side = {d: lax.ppermute(mine, plane, plane_perm(d, True)) for d in (1, -1, 2)}
    a, b = jnp.stack([mine, side[1]]), jnp.stack([side[-1], side[2]])
    far = lambda v, d: lax.ppermute(v, plane, plane_perm(d, False))
    left_a, right_b = far(a, 1), far(b, -1)
    left_b, right_a = far(b, 1), far(a, -1)
    sets = [a, b, left_a, left_b, right_a, right_b, far(left_a, 1), far(right_b, -1)]
    dk = jnp.array([k for k in STEPS for j in STEPS], jnp.int32)
    dj = jnp.array([j for k in STEPS for j in STEPS], jnp.int32)
    on_x = jnp.where(core == 0, dj, dk)
    on_y = jnp.where(core == 0, dk, dj)
    blk = ((y - on_y + 4) % 4) * 4 + (x - on_x + 4) % 4

    offs = jnp.arange(ROWS, dtype=jnp.int32)
    first_of = lambda c: (z * 2 + c) * ROWS
    lows, highs = [], []
    for c in (core, 1 - core):
        low, high = row_meta(first_of(c) + offs, doc_lengths, span_start, span_len)
        lows.append(low)
        highs.append(high)
    cosine, sine = angles(first_of(core) + offs - lows[0])
    lo, hi = jnp.stack(lows)[:, None, :], jnp.stack(highs)[:, None, :]
    slot = jnp.arange(16, dtype=jnp.int32)
    at = first_of(jnp.where(slot < 4, core, 1 - core)) + (slot % 2) * (ROWS - 1)
    low, high = row_meta(at, doc_lengths, span_start, span_len)
    meta = jnp.where(slot % 4 < 2, low, high)
    meta = jnp.where(slot == 8, z, jnp.where(slot == 9, core, meta)).astype(jnp.int32)

    w = jnp.concatenate([w_qkv[0], w_qkv[1], w_qkv[2]], axis=1)
    q, kv = project(blk, sets, w, cosine, sine)

    half = NZ // 2
    z_step = lambda v, d: lax.ppermute(v, "z", ring(NZ, d))
    put = lambda kvs, offs, state, **kw: attend(meta, q2, lo, hi, kvs, offs, state, **kw)
    up, down = z_step(kv, 1), z_step(kv, -1)
    up, q = lax.optimization_barrier((up, q))
    q2 = jnp.stack([q, lax.ppermute(q, "core", ring(2, 1))], axis=0)
    state, waiting = None, [([kv], [0])]
    for i in range(2, half + 1):
        waiting.append(([up, down], [1 - i, i - 1]))
        up = z_step(up, 1)
        if i < half:
            down = z_step(down, -1)
        for _ in range(1 if i < half else 2):
            state = put(*waiting.pop(0), state)
        up, state = lax.optimization_barrier((up, state))
    own, other = put([up], [-half], state, last_call=True)
    return merge(own, lax.ppermute(other, "core", ring(2, 1)))


def solution(mesh):
    fine = Mesh(mesh.devices.reshape(NZ, 2, 4, 4), ("z", "core", "y", "x"))
    both, plane = ("z", "core"), ("y", "x")
    return jax.shard_map(
        body,
        mesh=fine,
        in_specs=(P(both, plane), P(plane), P(None, None, plane), P(), P(), P()),
        out_specs=P(both, plane),
        check_vma=False,
    )
```

```python
import functools
import math

import jax
import jax.numpy as jnp
from jax import lax
from jax.experimental import pallas as pl
from jax.experimental.pallas import tpu as pltpu
from jax.sharding import Mesh, PartitionSpec as P

D = 4096
HD = 128
EPS = 1e-05
NEG = -1e30
ROWS = 512
FEAT = 256
PAD = 16
NZ = 16
C2 = math.log2(math.e) * HD**-0.5
STEPS = (0, 1, -1, 2)


def row_meta(idx, doc_lengths, span_start, span_len):
    starts = jnp.cumsum(doc_lengths) - doc_lengths
    mine = (idx[:, None] >= starts[None, :]) & (idx[:, None] < (starts + doc_lengths)[None, :])
    first = jnp.sum(jnp.where(mine, starts[None, :], 0), axis=1)
    last = jnp.sum(jnp.where(mine, (starts + doc_lengths)[None, :], 0), axis=1) - 1
    ends = span_start + span_len
    inside = (idx[:, None] >= span_start[None, :]) & (idx[:, None] < ends[None, :])
    reach = jnp.maximum(idx, jnp.max(jnp.where(inside, ends[None, :] - 1, 0), axis=1))
    return first, jnp.minimum(reach, last)


def angles(pos):
    half = HD // 2
    freqs = jnp.power(jnp.float32(500000.0), -2.0 * jnp.arange(half, dtype=jnp.float32) / HD)
    angle = pos.astype(jnp.float32)[:, None] * freqs[None, :]
    cosine = jnp.cos(angle)
    sine = jnp.sin(angle)
    return cosine, sine


def squares_and_scaled(sets, put):
    tile = 64
    count = 2 * len(sets)

    def rows_of(i, carry):
        r = pl.multiple_of(i * tile, tile)
        acc = jnp.zeros((tile, FEAT), jnp.float32)
        for b in range(count):
            x = sets[b // 2][b % 2, pl.ds(r, tile), :].astype(jnp.float32)
            gain = sets[b // 2][b % 2, ROWS : ROWS + 1, :].astype(jnp.float32)
            acc = acc + x * x
            put(b, r, tile, (x * gain).astype(jnp.bfloat16))
        put(None, r, tile, jnp.sum(acc, axis=1, keepdims=True))
        return carry

    lax.fori_loop(0, ROWS // tile, rows_of, 0)


def fetch_rows(blk_ref, first, count, w_ref, w_some, sem):
    fetches = []
    for b in range(count):
        row = pl.multiple_of(blk_ref[first + b] * FEAT, FEAT)
        for s in range(3):
            to = w_some.at[b * FEAT : (b + 1) * FEAT, s * HD : (s + 1) * HD]
            fetches.append(
                pltpu.make_async_copy(w_ref.at[s, pl.ds(row, FEAT), :], to, sem.at[3 * b + s])
            )
    for fetch in fetches:
        fetch.start()
    return fetches


def early_kernel(blk_ref, *refs):
    sets, (w_ref, out_ref, ssq_ref, xs, w_some, sem) = refs[:6], refs[6:]
    fetches = fetch_rows(blk_ref, 0, 12, w_ref, w_some, sem)

    def put(b, r, tile, value):
        if b is None:
            ssq_ref[pl.ds(r, tile), :] = jnp.broadcast_to(value, (tile, HD))
        else:
            xs[pl.ds(r, tile), b * FEAT : (b + 1) * FEAT] = value

    squares_and_scaled(sets, put)
    for fetch in fetches:
        fetch.wait()
    out_ref[...] = jnp.dot(xs[...], w_some[...], preferred_element_type=jnp.float32)


def late_kernel(blk_ref, *refs):
    sets = refs[:2]
    w_ref, out_ref, ssq_ref, cos_ref, sin_ref, q_ref, kv_ref, xs, ssq, w_some, sem = refs[2:]
    fetches = fetch_rows(blk_ref, 12, 4, w_ref, w_some, sem)

    def put(b, r, tile, value):
        if b is None:
            ssq[pl.ds(r, tile), :] = jnp.broadcast_to(value, (tile, HD))
        else:
            xs[pl.ds(r, tile), b * FEAT : (b + 1) * FEAT] = value

    squares_and_scaled(sets, put)
    for fetch in fetches:
        fetch.wait()
    out = out_ref[...] + jnp.dot(xs[...], w_some[...], preferred_element_type=jnp.float32)
    scale = lax.rsqrt((ssq_ref[...] + ssq[...]) / D + EPS)
    cosine = jnp.concatenate([cos_ref[...], cos_ref[...]], axis=1)
    sine = jnp.concatenate([-sin_ref[...], sin_ref[...]], axis=1)

    def rotate(v):
        v = v * scale
        return (v * cosine + pltpu.roll(v, HD // 2, 1) * sine).astype(jnp.bfloat16)

    q_ref[...] = rotate(out[:, :HD])
    kv_ref[:ROWS, :] = rotate(out[:, HD : 2 * HD])
    vt = (out[:, 2 * HD :] * scale).T.astype(jnp.bfloat16)
    for b in range(ROWS // HD):
        kv_ref[ROWS + b * HD : ROWS + (b + 1) * HD, :] = vt[:, b * HD : (b + 1) * HD]


def project(blk, sets, w, cosine, sine):
    vmem, smem = pl.BlockSpec(memory_space=pltpu.VMEM), pl.BlockSpec(memory_space=pltpu.SMEM)
    hbm = pl.BlockSpec(memory_space=pltpu.HBM)
    params = pltpu.CompilerParams(vmem_limit_bytes=20 * 2**20)
    cost = lambda blocks: pl.CostEstimate(
        flops=2 * ROWS * blocks * FEAT * 3 * HD, bytes_accessed=blocks * 2**19, transcendentals=0
    )
    out, ssq = pl.pallas_call(
        early_kernel,
        out_shape=(
            jax.ShapeDtypeStruct((ROWS, 3 * HD), jnp.float32),
            jax.ShapeDtypeStruct((ROWS, HD), jnp.float32),
        ),
        in_specs=[smem] + [vmem] * 6 + [hbm],
        out_specs=(vmem, vmem),
        scratch_shapes=[
            pltpu.VMEM((ROWS, 12 * FEAT), jnp.bfloat16),
            pltpu.VMEM((12 * FEAT, 3 * HD), jnp.bfloat16),
            pltpu.SemaphoreType.DMA((36,)),
        ],
        compiler_params=params,
        cost_estimate=cost(12),
        name="early_qkv",
    )(blk, *sets[:6], w)
    return pl.pallas_call(
        late_kernel,
        out_shape=(
            jax.ShapeDtypeStruct((ROWS, HD), jnp.bfloat16),
            jax.ShapeDtypeStruct((2 * ROWS, HD), jnp.bfloat16),
        ),
        in_specs=[smem] + [vmem] * 2 + [hbm] + [vmem] * 4,
        out_specs=(vmem, vmem),
        scratch_shapes=[
            pltpu.VMEM((ROWS, 4 * FEAT), jnp.bfloat16),
            pltpu.VMEM((ROWS, HD), jnp.float32),
            pltpu.VMEM((4 * FEAT, 3 * HD), jnp.bfloat16),
            pltpu.SemaphoreType.DMA((12,)),
        ],
        compiler_params=params,
        cost_estimate=cost(4),
        name="late_qkv",
    )(blk, *sets[6:], w, out, ssq, cosine, sine)


def attend_kernel(offs, fresh, last_call, meta_ref, q_ref, lo_ref, hi_ref, *refs):
    n = len(offs)
    kvs, st = refs[:n], refs[-1]
    if fresh:
        row = lax.broadcasted_iota(jnp.int32, st.shape, 1)
        st[...] = jnp.where(row == HD, NEG, 0.0)
    else:
        st[...] = refs[n][...]
    wide = 512
    per = ROWS // wide
    z, core = meta_ref[8], meta_ref[9]
    firsts = [
        (lax.rem(z + off + NZ, NZ) * 2 + core) * ROWS for off in offs
    ]

    def part(js, masked, i, carry):
        t = i // per
        cols = pl.ds(pl.multiple_of((i % per) * wide, wide), wide)
        query = q_ref[t, cols, :]
        ss = [
            lax.dot_general(
                kvs[j][:ROWS, :], query, (((1,), (1,)), ((), ())), preferred_element_type=jnp.float32
            )
            for j in js
        ]
        oks = [None] * len(js)
        if masked:
            lo, hi = lo_ref[t, :, cols], hi_ref[t, :, cols]
            row = lax.broadcasted_iota(jnp.int32, ss[0].shape, 0)
            oks = [(row >= lo - firsts[j]) & (row <= hi - firsts[j]) for j in js]
            ss = [jnp.where(ok, s, NEG) for ok, s in zip(oks, ss)]
        m_old = st[t, HD : HD + 1, cols]
        m_new = m_old
        for s in ss:
            m_new = jnp.maximum(m_new, jnp.max(s, axis=0, keepdims=True))
        alpha = jnp.exp2((m_old - m_new) * C2)
        total = st[t, HD + 1 : HD + 2, cols] * alpha
        acc = st[t, :HD, cols] * alpha
        shift = m_new * C2
        for j, s, ok in zip(js, ss, oks):
            p = jnp.exp2(s * C2 - shift)
            if masked:
                p = jnp.where(ok, p, 0.0)
            total = total + jnp.sum(p, axis=0, keepdims=True)
            vt = jnp.concatenate(
                [kvs[j][ROWS + b * HD : ROWS + (b + 1) * HD, :] for b in range(ROWS // HD)], axis=1
            )
            acc = acc + jnp.dot(vt, p.astype(jnp.bfloat16), preferred_element_type=jnp.float32)
        st[t, HD : HD + 1, cols] = m_new
        st[t, HD + 1 : HD + 2, cols] = total
        st[t, :HD, cols] = acc
        return carry

    needed, whole = {}, []
    for j in range(n):
        last = firsts[j] + ROWS - 1
        for t in range(2):
            needed[j, t] = (firsts[j] <= meta_ref[4 * t + 3]) & (last >= meta_ref[4 * t])
            whole.append((firsts[j] >= meta_ref[4 * t + 1]) & (last <= meta_ref[4 * t + 2]))
    every = functools.reduce(jnp.logical_and, whole)

    @pl.when(every)
    def _():
        lax.fori_loop(0, 2 * per, functools.partial(part, range(n), False), 0)

    for j in range(n):

        @pl.when(jnp.logical_not(every) & (needed[j, 0] | needed[j, 1]))
        def _(j=j):
            begin = jnp.where(needed[j, 0], 0, per)
            end = jnp.where(needed[j, 1], 2 * per, per)
            lax.fori_loop(begin, end, functools.partial(part, [j], True), 0)


    if last_call:
        for t in range(2):
            refs[-3 + t][...] = st[t]


def attend(meta, q, lo, hi, kvs, offs, state, last_call=False):
    n = len(kvs)
    vmem = pl.BlockSpec(memory_space=pltpu.VMEM)
    state = [] if state is None else [state]
    pairs = 2 * ROWS * ROWS * n
    full = (2, HD + 8, ROWS)
    part = jax.ShapeDtypeStruct(full[1:], jnp.float32)
    return pl.pallas_call(
        functools.partial(attend_kernel, offs, not state, last_call),
        out_shape=(part, part) if last_call else jax.ShapeDtypeStruct(full, jnp.float32),
        in_specs=[pl.BlockSpec(memory_space=pltpu.SMEM)] + [vmem] * (3 + n + len(state)),
        out_specs=(vmem, vmem) if last_call else vmem,
        scratch_shapes=[pltpu.VMEM(full, jnp.float32)] if last_call else [],
        input_output_aliases={4 + n: 0} if state and not last_call else {},
        compiler_params=pltpu.CompilerParams(vmem_limit_bytes=20 * 2**20),
        cost_estimate=pl.CostEstimate(
            flops=4 * pairs * HD, bytes_accessed=2 * 2**20, transcendentals=pairs
        ),
        name="attend",
    )(meta, q, lo, hi, *kvs, *state)


def merge_kernel(a_ref, b_ref, o_ref):
    ma, mb = a_ref[HD : HD + 1, :], b_ref[HD : HD + 1, :]
    m = jnp.maximum(ma, mb)
    wa, wb = jnp.exp2((ma - m) * C2), jnp.exp2((mb - m) * C2)
    total = a_ref[HD + 1 : HD + 2, :] * wa + b_ref[HD + 1 : HD + 2, :] * wb
    out = (a_ref[:HD, :] * wa + b_ref[:HD, :] * wb) / total
    o_ref[...] = out.T.astype(jnp.bfloat16)


def merge(a, b):
    vmem = pl.BlockSpec(memory_space=pltpu.VMEM)
    return pl.pallas_call(
        merge_kernel,
        out_shape=jax.ShapeDtypeStruct((ROWS, HD), jnp.bfloat16),
        in_specs=[vmem, vmem],
        out_specs=vmem,
        compiler_params=pltpu.CompilerParams(vmem_limit_bytes=4 * 2**20),
        name="merge",
    )(a, b)


def append_kernel(tok_ref, gain_ref, o_ref, gain, sem):
    rows = pltpu.make_async_copy(tok_ref, o_ref.at[:ROWS], sem.at[0])
    row = pltpu.make_async_copy(gain_ref, gain, sem.at[1])
    rows.start()
    row.start()
    row.wait()
    o_ref[ROWS:, :] = jnp.broadcast_to(gain[...][None, :], (PAD, FEAT))
    rows.wait()


def append(tokens, norm_gain):
    return pl.pallas_call(
        append_kernel,
        out_shape=jax.ShapeDtypeStruct((ROWS + PAD, FEAT), jnp.bfloat16),
        in_specs=[pl.BlockSpec(memory_space=pltpu.HBM)] * 2,
        out_specs=pl.BlockSpec(memory_space=pltpu.VMEM),
        scratch_shapes=[pltpu.VMEM((FEAT,), jnp.bfloat16), pltpu.SemaphoreType.DMA((2,))],
        compiler_params=pltpu.CompilerParams(vmem_limit_bytes=4 * 2**20),
        name="append",
    )(tokens, norm_gain)


def pair_kernel(u_ref, v_ref, o_ref, sem):
    copies = [
        pltpu.make_async_copy(ref, o_ref.at[i], sem.at[i]) for i, ref in enumerate((u_ref, v_ref))
    ]
    for copy in copies:
        copy.start()
    for copy in copies:
        copy.wait()


def pair(u, v):
    return pl.pallas_call(
        pair_kernel,
        out_shape=jax.ShapeDtypeStruct((2,) + u.shape, u.dtype),
        in_specs=[pl.BlockSpec(memory_space=pl.ANY)] * 2,
        out_specs=pl.BlockSpec(memory_space=pltpu.VMEM),
        scratch_shapes=[pltpu.SemaphoreType.DMA((2,))],
        compiler_params=pltpu.CompilerParams(vmem_limit_bytes=4 * 2**20),
        name="pair",
    )(u, v)


def plane_perm(d, first):
    out = []
    for c in range(2):
        for y in range(4):
            for x in range(4):
                if (c == 0) == first:
                    to = (y, (x + d) % 4)
                else:
                    to = ((y + d) % 4, x)
                out.append(((c * 4 + y) * 4 + x, (c * 4 + to[0]) * 4 + to[1]))
    return out


def ring(n, d):
    return [(i, (i + d) % n) for i in range(n)]


def body(tokens, norm_gain, w_qkv, doc_lengths, span_start, span_len):
    z, core = lax.axis_index("z"), lax.axis_index("core")
    y, x = lax.axis_index("y"), lax.axis_index("x")
    plane = ("core", "y", "x")

    mine = append(tokens, norm_gain)
    side = {d: lax.ppermute(mine, plane, plane_perm(d, True)) for d in (1, -1, 2)}
    a, b = pair(mine, side[1]), pair(side[-1], side[2])
    far = lambda v, d: lax.ppermute(v, plane, plane_perm(d, False))
    left_a, right_b = far(a, 1), far(b, -1)
    left_b, right_a = far(b, 1), far(a, -1)
    sets = [a, b, left_a, left_b, right_a, right_b, far(left_a, 1), far(right_b, -1)]
    dk = jnp.array([k for k in STEPS for j in STEPS], jnp.int32)
    dj = jnp.array([j for k in STEPS for j in STEPS], jnp.int32)
    on_x = jnp.where(core == 0, dj, dk)
    on_y = jnp.where(core == 0, dk, dj)
    blk = ((y - on_y + 4) % 4) * 4 + (x - on_x + 4) % 4

    offs = jnp.arange(ROWS, dtype=jnp.int32)
    first_of = lambda c: (z * 2 + c) * ROWS
    lows, highs = [], []
    for c in (core, 1 - core):
        low, high = row_meta(first_of(c) + offs, doc_lengths, span_start, span_len)
        lows.append(low)
        highs.append(high)
    cosine, sine = angles(first_of(core) + offs - lows[0])
    lo, hi = jnp.stack(lows)[:, None, :], jnp.stack(highs)[:, None, :]
    slot = jnp.arange(16, dtype=jnp.int32)
    at = first_of(jnp.where(slot < 4, core, 1 - core)) + (slot % 2) * (ROWS - 1)
    low, high = row_meta(at, doc_lengths, span_start, span_len)
    meta = jnp.where(slot % 4 < 2, low, high)
    meta = jnp.where(slot == 8, z, jnp.where(slot == 9, core, meta)).astype(jnp.int32)

    q, kv = project(blk, sets, w_qkv, cosine, sine)

    half = NZ // 2
    z_step = lambda v, d: lax.ppermute(v, "z", ring(NZ, d))
    put = lambda kvs, offs, state, **kw: attend(meta, q2, lo, hi, kvs, offs, state, **kw)
    up, down = z_step(kv, 1), z_step(kv, -1)
    up, q = lax.optimization_barrier((up, q))
    q2 = jnp.stack([q, lax.ppermute(q, "core", ring(2, 1))], axis=0)
    state, waiting = None, [([kv], [0])]
    for i in range(2, half + 1):
        waiting.append(([up, down], [1 - i, i - 1]))
        up = z_step(up, 1)
        if i < half:
            down = z_step(down, -1)
        for _ in range(1 if i < half else 2):
            state = put(*waiting.pop(0), state)
        up, state = lax.optimization_barrier((up, state))
    own, other = put([up], [-half], state, last_call=True)
    return merge(own, lax.ppermute(other, "core", ring(2, 1)))


def solution(mesh):
    fine = Mesh(mesh.devices.reshape(NZ, 2, 4, 4), ("z", "core", "y", "x"))
    both, plane = ("z", "core"), ("y", "x")
    return jax.shard_map(
        body,
        mesh=fine,
        in_specs=(P(both, plane), P(plane), P(None, None, plane), P(), P(), P()),
        out_specs=P(both, plane),
        check_vma=False,
    )
```

```python
import functools
import math

import jax
import jax.numpy as jnp
from jax import lax
from jax.experimental import pallas as pl
from jax.experimental.pallas import tpu as pltpu
from jax.sharding import Mesh, PartitionSpec as P

D = 4096
HD = 128
EPS = 1e-05
NEG = -1e30
ROWS = 512
FEAT = 256
PAD = 16
NZ = 16
C2 = math.log2(math.e) * HD**-0.5
STEPS = (0, 1, -1, 2)


def row_meta(idx, doc_lengths, span_start, span_len):
    starts = jnp.cumsum(doc_lengths) - doc_lengths
    mine = (idx[:, None] >= starts[None, :]) & (idx[:, None] < (starts + doc_lengths)[None, :])
    first = jnp.sum(jnp.where(mine, starts[None, :], 0), axis=1)
    last = jnp.sum(jnp.where(mine, (starts + doc_lengths)[None, :], 0), axis=1) - 1
    ends = span_start + span_len
    inside = (idx[:, None] >= span_start[None, :]) & (idx[:, None] < ends[None, :])
    reach = jnp.maximum(idx, jnp.max(jnp.where(inside, ends[None, :] - 1, 0), axis=1))
    return first, jnp.minimum(reach, last)


def angles(pos):
    half = HD // 2
    freqs = jnp.power(jnp.float32(500000.0), -2.0 * jnp.arange(half, dtype=jnp.float32) / HD)
    angle = pos.astype(jnp.float32)[:, None] * freqs[None, :]
    cosine = jnp.cos(angle)
    sine = jnp.sin(angle)
    return (
        jnp.concatenate([cosine, cosine], axis=1),
        jnp.concatenate([-sine, sine], axis=1),
    )


def qkv_kernel(blk_ref, *refs):
    sets, (w_ref, cos_ref, sin_ref, q_ref, kv_ref, nrm) = refs[:8], refs[8:]
    tile = 64

    def norm_rows(i, carry):
        r = pl.multiple_of(i * tile, tile)
        acc = jnp.zeros((tile, FEAT), jnp.float32)
        for b in range(16):
            x = sets[b // 2][b % 2, pl.ds(r, tile), :].astype(jnp.float32)
            acc = acc + x * x
        scale = lax.rsqrt(jnp.sum(acc, axis=1, keepdims=True) / D + EPS)
        for b in range(16):
            x = sets[b // 2][b % 2, pl.ds(r, tile), :].astype(jnp.float32)
            gain = sets[b // 2][b % 2, ROWS : ROWS + 1, :].astype(jnp.float32)
            col = pl.multiple_of(blk_ref[b] * FEAT, FEAT)
            nrm[pl.ds(r, tile), pl.ds(col, FEAT)] = (x * scale * gain).astype(jnp.bfloat16)
        return carry

    lax.fori_loop(0, ROWS // tile, norm_rows, 0)
    out = jnp.dot(nrm[...], w_ref[...], preferred_element_type=jnp.float32)
    cosine, sine = cos_ref[...], sin_ref[...]

    def rotate(v):
        return (v * cosine + pltpu.roll(v, HD // 2, 1) * sine).astype(jnp.bfloat16)

    q_ref[...] = rotate(out[:, :HD])
    kv_ref[:ROWS, :] = rotate(out[:, HD : 2 * HD])
    vt = out[:, 2 * HD :].T.astype(jnp.bfloat16)
    for b in range(ROWS // HD):
        kv_ref[ROWS + b * HD : ROWS + (b + 1) * HD, :] = vt[:, b * HD : (b + 1) * HD]


def project(blk, sets, w, cosine, sine):
    vmem = pl.BlockSpec(memory_space=pltpu.VMEM)
    return pl.pallas_call(
        qkv_kernel,
        out_shape=(
            jax.ShapeDtypeStruct((ROWS, HD), jnp.bfloat16),
            jax.ShapeDtypeStruct((2 * ROWS, HD), jnp.bfloat16),
        ),
        in_specs=[pl.BlockSpec(memory_space=pltpu.SMEM)] + [vmem] * 11,
        out_specs=(vmem, vmem),
        scratch_shapes=[pltpu.VMEM((ROWS, D), jnp.bfloat16)],
        compiler_params=pltpu.CompilerParams(vmem_limit_bytes=20 * 2**20),
        cost_estimate=pl.CostEstimate(
            flops=2 * ROWS * D * 3 * HD, bytes_accessed=8 * 2**20, transcendentals=0
        ),
        name="norm_qkv",
    )(blk, *sets, w, cosine, sine)


def attend_kernel(offs, fresh, last_call, meta_ref, q_ref, lo_ref, hi_ref, *refs):
    n = len(offs)
    kvs, st = refs[:n], refs[-1]
    if fresh:
        row = lax.broadcasted_iota(jnp.int32, st.shape, 1)
        st[...] = jnp.where(row == HD, NEG, 0.0)
    else:
        st[...] = refs[n][...]
    wide = 512
    per = ROWS // wide
    z, core = meta_ref[8], meta_ref[9]
    firsts = [
        (lax.rem(z + off + NZ, NZ) * 2 + core) * ROWS for off in offs
    ]

    def part(js, masked, i, carry):
        t = i // per
        cols = pl.ds(pl.multiple_of((i % per) * wide, wide), wide)
        query = q_ref[t, cols, :]
        ss = [
            lax.dot_general(
                kvs[j][:ROWS, :], query, (((1,), (1,)), ((), ())), preferred_element_type=jnp.float32
            )
            for j in js
        ]
        oks = [None] * len(js)
        if masked:
            lo, hi = lo_ref[t, :, cols], hi_ref[t, :, cols]
            row = lax.broadcasted_iota(jnp.int32, ss[0].shape, 0)
            oks = [(row >= lo - firsts[j]) & (row <= hi - firsts[j]) for j in js]
            ss = [jnp.where(ok, s, NEG) for ok, s in zip(oks, ss)]
        m_old = st[t, HD : HD + 1, cols]
        m_new = m_old
        for s in ss:
            m_new = jnp.maximum(m_new, jnp.max(s, axis=0, keepdims=True))
        alpha = jnp.exp2((m_old - m_new) * C2)
        total = st[t, HD + 1 : HD + 2, cols] * alpha
        acc = st[t, :HD, cols] * alpha
        shift = m_new * C2
        for j, s, ok in zip(js, ss, oks):
            p = jnp.exp2(s * C2 - shift)
            if masked:
                p = jnp.where(ok, p, 0.0)
            total = total + jnp.sum(p, axis=0, keepdims=True)
            vt = jnp.concatenate(
                [kvs[j][ROWS + b * HD : ROWS + (b + 1) * HD, :] for b in range(ROWS // HD)], axis=1
            )
            acc = acc + jnp.dot(vt, p.astype(jnp.bfloat16), preferred_element_type=jnp.float32)
        st[t, HD : HD + 1, cols] = m_new
        st[t, HD + 1 : HD + 2, cols] = total
        st[t, :HD, cols] = acc
        return carry

    needed, whole = {}, []
    for j in range(n):
        last = firsts[j] + ROWS - 1
        for t in range(2):
            needed[j, t] = (firsts[j] <= meta_ref[4 * t + 3]) & (last >= meta_ref[4 * t])
            whole.append((firsts[j] >= meta_ref[4 * t + 1]) & (last <= meta_ref[4 * t + 2]))
    every = functools.reduce(jnp.logical_and, whole)

    @pl.when(every)
    def _():
        lax.fori_loop(0, 2 * per, functools.partial(part, range(n), False), 0)

    for j in range(n):

        @pl.when(jnp.logical_not(every) & (needed[j, 0] | needed[j, 1]))
        def _(j=j):
            begin = jnp.where(needed[j, 0], 0, per)
            end = jnp.where(needed[j, 1], 2 * per, per)
            lax.fori_loop(begin, end, functools.partial(part, [j], True), 0)


    if last_call:
        for t in range(2):
            refs[-3 + t][...] = st[t]


def attend(meta, q, lo, hi, kvs, offs, state, last_call=False):
    n = len(kvs)
    vmem = pl.BlockSpec(memory_space=pltpu.VMEM)
    state = [] if state is None else [state]
    pairs = 2 * ROWS * ROWS * n
    full = (2, HD + 8, ROWS)
    part = jax.ShapeDtypeStruct(full[1:], jnp.float32)
    return pl.pallas_call(
        functools.partial(attend_kernel, offs, not state, last_call),
        out_shape=(part, part) if last_call else jax.ShapeDtypeStruct(full, jnp.float32),
        in_specs=[pl.BlockSpec(memory_space=pltpu.SMEM)] + [vmem] * (3 + n + len(state)),
        out_specs=(vmem, vmem) if last_call else vmem,
        scratch_shapes=[pltpu.VMEM(full, jnp.float32)] if last_call else [],
        input_output_aliases={4 + n: 0} if state and not last_call else {},
        compiler_params=pltpu.CompilerParams(vmem_limit_bytes=20 * 2**20),
        cost_estimate=pl.CostEstimate(
            flops=4 * pairs * HD, bytes_accessed=2 * 2**20, transcendentals=pairs
        ),
        name="attend",
    )(meta, q, lo, hi, *kvs, *state)


def merge_kernel(a_ref, b_ref, o_ref):
    ma, mb = a_ref[HD : HD + 1, :], b_ref[HD : HD + 1, :]
    m = jnp.maximum(ma, mb)
    wa, wb = jnp.exp2((ma - m) * C2), jnp.exp2((mb - m) * C2)
    total = a_ref[HD + 1 : HD + 2, :] * wa + b_ref[HD + 1 : HD + 2, :] * wb
    out = (a_ref[:HD, :] * wa + b_ref[:HD, :] * wb) / total
    o_ref[...] = out.T.astype(jnp.bfloat16)


def merge(a, b):
    vmem = pl.BlockSpec(memory_space=pltpu.VMEM)
    return pl.pallas_call(
        merge_kernel,
        out_shape=jax.ShapeDtypeStruct((ROWS, HD), jnp.bfloat16),
        in_specs=[vmem, vmem],
        out_specs=vmem,
        compiler_params=pltpu.CompilerParams(vmem_limit_bytes=4 * 2**20),
        name="merge",
    )(a, b)


def plane_perm(d, first):
    out = []
    for c in range(2):
        for y in range(4):
            for x in range(4):
                if (c == 0) == first:
                    to = (y, (x + d) % 4)
                else:
                    to = ((y + d) % 4, x)
                out.append(((c * 4 + y) * 4 + x, (c * 4 + to[0]) * 4 + to[1]))
    return out


def ring(n, d):
    return [(i, (i + d) % n) for i in range(n)]


def body(tokens, norm_gain, w_qkv, doc_lengths, span_start, span_len):
    z, core = lax.axis_index("z"), lax.axis_index("core")
    y, x = lax.axis_index("y"), lax.axis_index("x")
    plane = ("core", "y", "x")

    mine = jnp.concatenate([tokens, jnp.broadcast_to(norm_gain[None, :], (PAD, FEAT))], axis=0)
    side = {d: lax.ppermute(mine, plane, plane_perm(d, True)) for d in (1, -1, 2)}
    a, b = jnp.stack([mine, side[1]]), jnp.stack([side[-1], side[2]])
    far = lambda v, d: lax.ppermute(v, plane, plane_perm(d, False))
    left_a, right_b = far(a, 1), far(b, -1)
    left_b, right_a = far(b, 1), far(a, -1)
    sets = [a, b, left_a, left_b, right_a, right_b, far(left_a, 1), far(right_b, -1)]
    dk = jnp.array([k for k in STEPS for j in STEPS], jnp.int32)
    dj = jnp.array([j for k in STEPS for j in STEPS], jnp.int32)
    on_x = jnp.where(core == 0, dj, dk)
    on_y = jnp.where(core == 0, dk, dj)
    blk = ((y - on_y + 4) % 4) * 4 + (x - on_x + 4) % 4

    offs = jnp.arange(ROWS, dtype=jnp.int32)
    first_of = lambda c: (z * 2 + c) * ROWS
    lows, highs = [], []
    for c in (core, 1 - core):
        low, high = row_meta(first_of(c) + offs, doc_lengths, span_start, span_len)
        lows.append(low)
        highs.append(high)
    cosine, sine = angles(first_of(core) + offs - lows[0])
    lo, hi = jnp.stack(lows)[:, None, :], jnp.stack(highs)[:, None, :]
    slot = jnp.arange(16, dtype=jnp.int32)
    at = first_of(jnp.where(slot < 4, core, 1 - core)) + (slot % 2) * (ROWS - 1)
    low, high = row_meta(at, doc_lengths, span_start, span_len)
    meta = jnp.where(slot % 4 < 2, low, high)
    meta = jnp.where(slot == 8, z, jnp.where(slot == 9, core, meta)).astype(jnp.int32)

    w = jnp.concatenate([w_qkv[0], w_qkv[1], w_qkv[2]], axis=1)
    q, kv = project(blk, sets, w, cosine, sine)

    half = NZ // 2
    z_step = lambda v, d: lax.ppermute(v, "z", ring(NZ, d))
    put = lambda kvs, offs, state, **kw: attend(meta, q2, lo, hi, kvs, offs, state, **kw)
    up, down = z_step(kv, 1), z_step(kv, -1)
    up, q = lax.optimization_barrier((up, q))
    q2 = jnp.stack([q, lax.ppermute(q, "core", ring(2, 1))], axis=0)
    state, waiting = None, [([kv], [0])]
    for i in range(2, half + 1):
        waiting.append(([up, down], [1 - i, i - 1]))
        up = z_step(up, 1)
        if i < half:
            down = z_step(down, -1)
        for _ in range(1 if i < half else 2):
            state = put(*waiting.pop(0), state)
        up, state = lax.optimization_barrier((up, state))
    own, other = put([up], [-half], state, last_call=True)
    return merge(own, lax.ppermute(other, "core", ring(2, 1)))


def solution(mesh):
    fine = Mesh(mesh.devices.reshape(NZ, 2, 4, 4), ("z", "core", "y", "x"))
    both, plane = ("z", "core"), ("y", "x")
    return jax.shard_map(
        body,
        mesh=fine,
        in_specs=(P(both, plane), P(plane), P(None, None, plane), P(), P(), P()),
        out_specs=P(both, plane),
        check_vma=False,
    )
```

```python
import functools
import math

import jax
import jax.numpy as jnp
from jax import lax
from jax.experimental import pallas as pl
from jax.experimental.pallas import tpu as pltpu
from jax.sharding import Mesh, PartitionSpec as P

D = 4096
HD = 128
EPS = 1e-05
NEG = -1e30
ROWS = 512
FEAT = 256
PAD = 16
NZ = 16
C2 = math.log2(math.e) * HD**-0.5
STEPS = (0, 1, -1, 2)


def row_meta(idx, doc_lengths, span_start, span_len):
    starts = jnp.cumsum(doc_lengths) - doc_lengths
    mine = (idx[:, None] >= starts[None, :]) & (idx[:, None] < (starts + doc_lengths)[None, :])
    first = jnp.sum(jnp.where(mine, starts[None, :], 0), axis=1)
    last = jnp.sum(jnp.where(mine, (starts + doc_lengths)[None, :], 0), axis=1) - 1
    ends = span_start + span_len
    inside = (idx[:, None] >= span_start[None, :]) & (idx[:, None] < ends[None, :])
    reach = jnp.maximum(idx, jnp.max(jnp.where(inside, ends[None, :] - 1, 0), axis=1))
    return first, jnp.minimum(reach, last)


def angles(pos):
    half = HD // 2
    freqs = jnp.power(jnp.float32(500000.0), -2.0 * jnp.arange(half, dtype=jnp.float32) / HD)
    angle = pos.astype(jnp.float32)[:, None] * freqs[None, :]
    cosine = jnp.cos(angle)
    sine = jnp.sin(angle)
    return (
        jnp.concatenate([cosine, cosine], axis=1),
        jnp.concatenate([-sine, sine], axis=1),
    )


def qkv_kernel(blk_ref, *refs):
    sets = refs[:8]
    w_ref, cos_ref, sin_ref, q_ref, kv_ref, scale_ref = refs[8:14]
    parts = refs[14:]
    tile = 64

    def squares(i, carry):
        r = pl.ds(pl.multiple_of(i * tile, tile), tile)
        acc = jnp.zeros((tile, FEAT), jnp.float32)
        for b in range(16):
            x = sets[b // 2][b % 2, r, :].astype(jnp.float32)
            acc = acc + x * x
        scale = lax.rsqrt(jnp.sum(acc, axis=1, keepdims=True) / D + EPS)
        scale_ref[r, :] = jnp.broadcast_to(scale, (tile, HD))
        return carry

    lax.fori_loop(0, ROWS // tile, squares, 0)
    scale = jnp.concatenate([scale_ref[...], scale_ref[...]], axis=1)

    def fill(g):
        for j in range(4):
            blocks = sets[2 * g + j // 2]
            x = blocks[j % 2, :ROWS, :].astype(jnp.float32)
            gain = blocks[j % 2, ROWS : ROWS + 1, :].astype(jnp.float32)
            parts[g][:, j * FEAT : (j + 1) * FEAT] = (x * scale * gain).astype(jnp.bfloat16)

    fill(0)
    out = None
    for g in range(4):
        rows = [pl.multiple_of(blk_ref[4 * g + j] * FEAT, FEAT) for j in range(4)]
        w = jnp.concatenate([w_ref[pl.ds(row, FEAT), :] for row in rows], axis=0)
        part = jnp.dot(parts[g][...], w, preferred_element_type=jnp.float32)
        if g < 3:
            fill(g + 1)
        out = part if g == 0 else out + part
    cosine, sine = cos_ref[...], sin_ref[...]

    def rotate(v):
        return (v * cosine + pltpu.roll(v, HD // 2, 1) * sine).astype(jnp.bfloat16)

    q_ref[...] = rotate(out[:, :HD])
    kv_ref[:ROWS, :] = rotate(out[:, HD : 2 * HD])
    vt = out[:, 2 * HD :].T.astype(jnp.bfloat16)
    for b in range(ROWS // HD):
        kv_ref[ROWS + b * HD : ROWS + (b + 1) * HD, :] = vt[:, b * HD : (b + 1) * HD]


def project(blk, sets, w, cosine, sine):
    vmem = pl.BlockSpec(memory_space=pltpu.VMEM)
    return pl.pallas_call(
        qkv_kernel,
        out_shape=(
            jax.ShapeDtypeStruct((ROWS, HD), jnp.bfloat16),
            jax.ShapeDtypeStruct((2 * ROWS, HD), jnp.bfloat16),
        ),
        in_specs=[pl.BlockSpec(memory_space=pltpu.SMEM)] + [vmem] * 11,
        out_specs=(vmem, vmem),
        scratch_shapes=[pltpu.VMEM((ROWS, HD), jnp.float32)]
        + [pltpu.VMEM((ROWS, 4 * FEAT), jnp.bfloat16)] * 4,
        compiler_params=pltpu.CompilerParams(vmem_limit_bytes=20 * 2**20),
        cost_estimate=pl.CostEstimate(
            flops=2 * ROWS * D * 3 * HD, bytes_accessed=8 * 2**20, transcendentals=0
        ),
        name="norm_qkv",
    )(blk, *sets, w, cosine, sine)


def attend_kernel(offs, fresh, last_call, meta_ref, q_ref, lo_ref, hi_ref, *refs):
    n = len(offs)
    kvs, st = refs[:n], refs[-1]
    if fresh:
        row = lax.broadcasted_iota(jnp.int32, st.shape, 1)
        st[...] = jnp.where(row == HD, NEG, 0.0)
    else:
        st[...] = refs[n][...]
    wide = 512
    per = ROWS // wide
    z, core = meta_ref[8], meta_ref[9]
    firsts = [
        (lax.rem(z + off + NZ, NZ) * 2 + core) * ROWS for off in offs
    ]

    def part(js, masked, i, carry):
        t = i // per
        cols = pl.ds(pl.multiple_of((i % per) * wide, wide), wide)
        query = q_ref[t, cols, :]
        ss = [
            lax.dot_general(
                kvs[j][:ROWS, :], query, (((1,), (1,)), ((), ())), preferred_element_type=jnp.float32
            )
            for j in js
        ]
        oks = [None] * len(js)
        if masked:
            lo, hi = lo_ref[t, :, cols], hi_ref[t, :, cols]
            row = lax.broadcasted_iota(jnp.int32, ss[0].shape, 0)
            oks = [(row >= lo - firsts[j]) & (row <= hi - firsts[j]) for j in js]
            ss = [jnp.where(ok, s, NEG) for ok, s in zip(oks, ss)]
        m_old = st[t, HD : HD + 1, cols]
        m_new = m_old
        for s in ss:
            m_new = jnp.maximum(m_new, jnp.max(s, axis=0, keepdims=True))
        alpha = jnp.exp2((m_old - m_new) * C2)
        total = st[t, HD + 1 : HD + 2, cols] * alpha
        acc = st[t, :HD, cols] * alpha
        shift = m_new * C2
        for j, s, ok in zip(js, ss, oks):
            p = jnp.exp2(s * C2 - shift)
            if masked:
                p = jnp.where(ok, p, 0.0)
            total = total + jnp.sum(p, axis=0, keepdims=True)
            vt = jnp.concatenate(
                [kvs[j][ROWS + b * HD : ROWS + (b + 1) * HD, :] for b in range(ROWS // HD)], axis=1
            )
            acc = acc + jnp.dot(vt, p.astype(jnp.bfloat16), preferred_element_type=jnp.float32)
        st[t, HD : HD + 1, cols] = m_new
        st[t, HD + 1 : HD + 2, cols] = total
        st[t, :HD, cols] = acc
        return carry

    needed, whole = {}, []
    for j in range(n):
        last = firsts[j] + ROWS - 1
        for t in range(2):
            needed[j, t] = (firsts[j] <= meta_ref[4 * t + 3]) & (last >= meta_ref[4 * t])
            whole.append((firsts[j] >= meta_ref[4 * t + 1]) & (last <= meta_ref[4 * t + 2]))
    every = functools.reduce(jnp.logical_and, whole)

    @pl.when(every)
    def _():
        lax.fori_loop(0, 2 * per, functools.partial(part, range(n), False), 0)

    for j in range(n):

        @pl.when(jnp.logical_not(every) & (needed[j, 0] | needed[j, 1]))
        def _(j=j):
            begin = jnp.where(needed[j, 0], 0, per)
            end = jnp.where(needed[j, 1], 2 * per, per)
            lax.fori_loop(begin, end, functools.partial(part, [j], True), 0)


    if last_call:
        for t in range(2):
            refs[-3 + t][...] = st[t]


def attend(meta, q, lo, hi, kvs, offs, state, last_call=False):
    n = len(kvs)
    vmem = pl.BlockSpec(memory_space=pltpu.VMEM)
    state = [] if state is None else [state]
    pairs = 2 * ROWS * ROWS * n
    full = (2, HD + 8, ROWS)
    part = jax.ShapeDtypeStruct(full[1:], jnp.float32)
    return pl.pallas_call(
        functools.partial(attend_kernel, offs, not state, last_call),
        out_shape=(part, part) if last_call else jax.ShapeDtypeStruct(full, jnp.float32),
        in_specs=[pl.BlockSpec(memory_space=pltpu.SMEM)] + [vmem] * (3 + n + len(state)),
        out_specs=(vmem, vmem) if last_call else vmem,
        scratch_shapes=[pltpu.VMEM(full, jnp.float32)] if last_call else [],
        input_output_aliases={4 + n: 0} if state and not last_call else {},
        compiler_params=pltpu.CompilerParams(vmem_limit_bytes=20 * 2**20),
        cost_estimate=pl.CostEstimate(
            flops=4 * pairs * HD, bytes_accessed=2 * 2**20, transcendentals=pairs
        ),
        name="attend",
    )(meta, q, lo, hi, *kvs, *state)


def merge_kernel(a_ref, b_ref, o_ref):
    ma, mb = a_ref[HD : HD + 1, :], b_ref[HD : HD + 1, :]
    m = jnp.maximum(ma, mb)
    wa, wb = jnp.exp2((ma - m) * C2), jnp.exp2((mb - m) * C2)
    total = a_ref[HD + 1 : HD + 2, :] * wa + b_ref[HD + 1 : HD + 2, :] * wb
    out = (a_ref[:HD, :] * wa + b_ref[:HD, :] * wb) / total
    o_ref[...] = out.T.astype(jnp.bfloat16)


def merge(a, b):
    vmem = pl.BlockSpec(memory_space=pltpu.VMEM)
    return pl.pallas_call(
        merge_kernel,
        out_shape=jax.ShapeDtypeStruct((ROWS, HD), jnp.bfloat16),
        in_specs=[vmem, vmem],
        out_specs=vmem,
        compiler_params=pltpu.CompilerParams(vmem_limit_bytes=4 * 2**20),
        name="merge",
    )(a, b)


def plane_perm(d, first):
    out = []
    for c in range(2):
        for y in range(4):
            for x in range(4):
                if (c == 0) == first:
                    to = (y, (x + d) % 4)
                else:
                    to = ((y + d) % 4, x)
                out.append(((c * 4 + y) * 4 + x, (c * 4 + to[0]) * 4 + to[1]))
    return out


def ring(n, d):
    return [(i, (i + d) % n) for i in range(n)]


def body(tokens, norm_gain, w_qkv, doc_lengths, span_start, span_len):
    z, core = lax.axis_index("z"), lax.axis_index("core")
    y, x = lax.axis_index("y"), lax.axis_index("x")
    plane = ("core", "y", "x")

    mine = jnp.concatenate([tokens, jnp.broadcast_to(norm_gain[None, :], (PAD, FEAT))], axis=0)
    side = {d: lax.ppermute(mine, plane, plane_perm(d, True)) for d in (1, -1, 2)}
    a, b = jnp.stack([mine, side[1]]), jnp.stack([side[-1], side[2]])
    far = lambda v, d: lax.ppermute(v, plane, plane_perm(d, False))
    left_a, right_b = far(a, 1), far(b, -1)
    left_b, right_a = far(b, 1), far(a, -1)
    sets = [a, b, left_a, left_b, right_a, right_b, far(left_a, 1), far(right_b, -1)]
    dk = jnp.array([k for k in STEPS for j in STEPS], jnp.int32)
    dj = jnp.array([j for k in STEPS for j in STEPS], jnp.int32)
    on_x = jnp.where(core == 0, dj, dk)
    on_y = jnp.where(core == 0, dk, dj)
    blk = ((y - on_y + 4) % 4) * 4 + (x - on_x + 4) % 4

    offs = jnp.arange(ROWS, dtype=jnp.int32)
    first_of = lambda c: (z * 2 + c) * ROWS
    lows, highs = [], []
    for c in (core, 1 - core):
        low, high = row_meta(first_of(c) + offs, doc_lengths, span_start, span_len)
        lows.append(low)
        highs.append(high)
    cosine, sine = angles(first_of(core) + offs - lows[0])
    lo, hi = jnp.stack(lows)[:, None, :], jnp.stack(highs)[:, None, :]
    slot = jnp.arange(16, dtype=jnp.int32)
    at = first_of(jnp.where(slot < 4, core, 1 - core)) + (slot % 2) * (ROWS - 1)
    low, high = row_meta(at, doc_lengths, span_start, span_len)
    meta = jnp.where(slot % 4 < 2, low, high)
    meta = jnp.where(slot == 8, z, jnp.where(slot == 9, core, meta)).astype(jnp.int32)

    w = jnp.concatenate([w_qkv[0], w_qkv[1], w_qkv[2]], axis=1)
    q, kv = project(blk, sets, w, cosine, sine)

    half = NZ // 2
    z_step = lambda v, d: lax.ppermute(v, "z", ring(NZ, d))
    put = lambda kvs, offs, state, **kw: attend(meta, q2, lo, hi, kvs, offs, state, **kw)
    up, down = z_step(kv, 1), z_step(kv, -1)
    up, q = lax.optimization_barrier((up, q))
    q2 = jnp.stack([q, lax.ppermute(q, "core", ring(2, 1))], axis=0)
    state, waiting = None, [([kv], [0])]
    for i in range(2, half + 1):
        waiting.append(([up, down], [1 - i, i - 1]))
        up = z_step(up, 1)
        if i < half:
            down = z_step(down, -1)
        for _ in range(1 if i < half else 2):
            state = put(*waiting.pop(0), state)
        up, state = lax.optimization_barrier((up, state))
    own, other = put([up], [-half], state, last_call=True)
    return merge(own, lax.ppermute(other, "core", ring(2, 1)))


def solution(mesh):
    fine = Mesh(mesh.devices.reshape(NZ, 2, 4, 4), ("z", "core", "y", "x"))
    both, plane = ("z", "core"), ("y", "x")
    return jax.shard_map(
        body,
        mesh=fine,
        in_specs=(P(both, plane), P(plane), P(None, None, plane), P(), P(), P()),
        out_specs=P(both, plane),
        check_vma=False,
    )
```

```python
import functools
import math

import jax
import jax.numpy as jnp
from jax import lax
from jax.experimental import pallas as pl
from jax.experimental.pallas import tpu as pltpu
from jax.sharding import Mesh, PartitionSpec as P

D = 4096
HD = 128
EPS = 1e-05
NEG = -1e30
ROWS = 512
FEAT = 256
PAD = 16
NZ = 16
C2 = math.log2(math.e) * HD**-0.5
STEPS = (0, 1, -1, 2)


def row_meta(idx, doc_lengths, span_start, span_len):
    starts = jnp.cumsum(doc_lengths) - doc_lengths
    mine = (idx[:, None] >= starts[None, :]) & (idx[:, None] < (starts + doc_lengths)[None, :])
    first = jnp.sum(jnp.where(mine, starts[None, :], 0), axis=1)
    last = jnp.sum(jnp.where(mine, (starts + doc_lengths)[None, :], 0), axis=1) - 1
    ends = span_start + span_len
    inside = (idx[:, None] >= span_start[None, :]) & (idx[:, None] < ends[None, :])
    reach = jnp.maximum(idx, jnp.max(jnp.where(inside, ends[None, :] - 1, 0), axis=1))
    return first, jnp.minimum(reach, last)


def angles(pos):
    half = HD // 2
    freqs = jnp.power(jnp.float32(500000.0), -2.0 * jnp.arange(half, dtype=jnp.float32) / HD)
    angle = pos.astype(jnp.float32)[:, None] * freqs[None, :]
    cosine = jnp.cos(angle)
    sine = jnp.sin(angle)
    return (
        jnp.concatenate([cosine, cosine], axis=1),
        jnp.concatenate([-sine, sine], axis=1),
    )


def qkv_kernel(blk_ref, *refs):
    sets = refs[:8]
    w_ref, cos_ref, sin_ref, q_ref, kv_ref, scale_ref = refs[8:14]
    parts = refs[14:]
    tile = 64

    def squares(i, carry):
        r = pl.ds(pl.multiple_of(i * tile, tile), tile)
        acc = jnp.zeros((tile, FEAT), jnp.float32)
        for b in range(16):
            x = sets[b // 2][b % 2, r, :].astype(jnp.float32)
            acc = acc + x * x
        scale = lax.rsqrt(jnp.sum(acc, axis=1, keepdims=True) / D + EPS)
        scale_ref[r, :] = jnp.broadcast_to(scale, (tile, HD))
        return carry

    lax.fori_loop(0, ROWS // tile, squares, 0)
    scale = jnp.concatenate([scale_ref[...], scale_ref[...]], axis=1)

    def fill(g):
        for j in range(4):
            blocks = sets[2 * g + j // 2]
            x = blocks[j % 2, :ROWS, :].astype(jnp.float32)
            gain = blocks[j % 2, ROWS : ROWS + 1, :].astype(jnp.float32)
            parts[g][:, j * FEAT : (j + 1) * FEAT] = (x * scale * gain).astype(jnp.bfloat16)

    fill(0)
    out = None
    for g in range(4):
        rows = [pl.multiple_of(blk_ref[4 * g + j] * FEAT, FEAT) for j in range(4)]
        w = jnp.concatenate([w_ref[pl.ds(row, FEAT), :] for row in rows], axis=0)
        part = jnp.dot(parts[g][...], w, preferred_element_type=jnp.float32)
        if g < 3:
            fill(g + 1)
        out = part if g == 0 else out + part
    cosine, sine = cos_ref[...], sin_ref[...]

    def rotate(v):
        return (v * cosine + pltpu.roll(v, HD // 2, 1) * sine).astype(jnp.bfloat16)

    q_ref[...] = rotate(out[:, :HD])
    kv_ref[:ROWS, :] = rotate(out[:, HD : 2 * HD])
    vt = out[:, 2 * HD :].T.astype(jnp.bfloat16)
    for b in range(ROWS // HD):
        kv_ref[ROWS + b * HD : ROWS + (b + 1) * HD, :] = vt[:, b * HD : (b + 1) * HD]


def project(blk, sets, w, cosine, sine):
    vmem = pl.BlockSpec(memory_space=pltpu.VMEM)
    return pl.pallas_call(
        qkv_kernel,
        out_shape=(
            jax.ShapeDtypeStruct((ROWS, HD), jnp.bfloat16),
            jax.ShapeDtypeStruct((2 * ROWS, HD), jnp.bfloat16),
        ),
        in_specs=[pl.BlockSpec(memory_space=pltpu.SMEM)] + [vmem] * 11,
        out_specs=(vmem, vmem),
        scratch_shapes=[pltpu.VMEM((ROWS, HD), jnp.float32)]
        + [pltpu.VMEM((ROWS, 4 * FEAT), jnp.bfloat16)] * 4,
        compiler_params=pltpu.CompilerParams(vmem_limit_bytes=20 * 2**20),
        cost_estimate=pl.CostEstimate(
            flops=2 * ROWS * D * 3 * HD, bytes_accessed=8 * 2**20, transcendentals=0
        ),
        name="norm_qkv",
    )(blk, *sets, w, cosine, sine)


def attend_kernel(offs, fresh, last_call, meta_ref, q_ref, lo_ref, hi_ref, *refs):
    n = len(offs)
    kvs, st = refs[:n], refs[-1]
    if fresh:
        row = lax.broadcasted_iota(jnp.int32, st.shape, 1)
        st[...] = jnp.where(row == HD, NEG, 0.0)
    else:
        st[...] = refs[n][...]
    wide = 512
    per = ROWS // wide
    z, core = meta_ref[8], meta_ref[9]
    firsts = [
        (lax.rem(z + off + NZ, NZ) * 2 + core) * ROWS for off in offs
    ]

    def part(js, masked, i, carry):
        t = i // per
        cols = pl.ds(pl.multiple_of((i % per) * wide, wide), wide)
        query = q_ref[t, cols, :]
        ss = [
            lax.dot_general(
                kvs[j][:ROWS, :], query, (((1,), (1,)), ((), ())), preferred_element_type=jnp.float32
            )
            for j in js
        ]
        oks = [None] * len(js)
        if masked:
            lo, hi = lo_ref[t, :, cols], hi_ref[t, :, cols]
            row = lax.broadcasted_iota(jnp.int32, ss[0].shape, 0)
            oks = [(row >= lo - firsts[j]) & (row <= hi - firsts[j]) for j in js]
            ss = [jnp.where(ok, s, NEG) for ok, s in zip(oks, ss)]
        m_old = st[t, HD : HD + 1, cols]
        m_new = m_old
        for s in ss:
            m_new = jnp.maximum(m_new, jnp.max(s, axis=0, keepdims=True))
        alpha = jnp.exp2((m_old - m_new) * C2)
        total = st[t, HD + 1 : HD + 2, cols] * alpha
        acc = st[t, :HD, cols] * alpha
        shift = jnp.maximum(m_new, 0.1 * NEG) * C2
        for j, s in zip(js, ss):
            p = jnp.exp2(s * C2 - shift)
            total = total + jnp.sum(p, axis=0, keepdims=True)
            vt = jnp.concatenate(
                [kvs[j][ROWS + b * HD : ROWS + (b + 1) * HD, :] for b in range(ROWS // HD)], axis=1
            )
            acc = acc + jnp.dot(vt, p.astype(jnp.bfloat16), preferred_element_type=jnp.float32)
        st[t, HD : HD + 1, cols] = m_new
        st[t, HD + 1 : HD + 2, cols] = total
        st[t, :HD, cols] = acc
        return carry

    needed, whole = {}, []
    for j in range(n):
        last = firsts[j] + ROWS - 1
        for t in range(2):
            needed[j, t] = (firsts[j] <= meta_ref[4 * t + 3]) & (last >= meta_ref[4 * t])
            whole.append((firsts[j] >= meta_ref[4 * t + 1]) & (last <= meta_ref[4 * t + 2]))
    every = functools.reduce(jnp.logical_and, whole)

    @pl.when(every)
    def _():
        lax.fori_loop(0, 2 * per, functools.partial(part, range(n), False), 0)

    for j in range(n):

        @pl.when(jnp.logical_not(every) & (needed[j, 0] | needed[j, 1]))
        def _(j=j):
            begin = jnp.where(needed[j, 0], 0, per)
            end = jnp.where(needed[j, 1], 2 * per, per)
            lax.fori_loop(begin, end, functools.partial(part, [j], True), 0)


    if last_call:
        for t in range(2):
            refs[-3 + t][...] = st[t]


def attend(meta, q, lo, hi, kvs, offs, state, last_call=False):
    n = len(kvs)
    vmem = pl.BlockSpec(memory_space=pltpu.VMEM)
    state = [] if state is None else [state]
    pairs = 2 * ROWS * ROWS * n
    full = (2, HD + 8, ROWS)
    part = jax.ShapeDtypeStruct(full[1:], jnp.float32)
    return pl.pallas_call(
        functools.partial(attend_kernel, offs, not state, last_call),
        out_shape=(part, part) if last_call else jax.ShapeDtypeStruct(full, jnp.float32),
        in_specs=[pl.BlockSpec(memory_space=pltpu.SMEM)] + [vmem] * (3 + n + len(state)),
        out_specs=(vmem, vmem) if last_call else vmem,
        scratch_shapes=[pltpu.VMEM(full, jnp.float32)] if last_call else [],
        input_output_aliases={4 + n: 0} if state and not last_call else {},
        compiler_params=pltpu.CompilerParams(vmem_limit_bytes=20 * 2**20),
        cost_estimate=pl.CostEstimate(
            flops=4 * pairs * HD, bytes_accessed=2 * 2**20, transcendentals=pairs
        ),
        name="attend",
    )(meta, q, lo, hi, *kvs, *state)


def merge_kernel(a_ref, b_ref, o_ref):
    ma, mb = a_ref[HD : HD + 1, :], b_ref[HD : HD + 1, :]
    m = jnp.maximum(ma, mb)
    wa, wb = jnp.exp2((ma - m) * C2), jnp.exp2((mb - m) * C2)
    total = a_ref[HD + 1 : HD + 2, :] * wa + b_ref[HD + 1 : HD + 2, :] * wb
    out = (a_ref[:HD, :] * wa + b_ref[:HD, :] * wb) / total
    o_ref[...] = out.T.astype(jnp.bfloat16)


def merge(a, b):
    vmem = pl.BlockSpec(memory_space=pltpu.VMEM)
    return pl.pallas_call(
        merge_kernel,
        out_shape=jax.ShapeDtypeStruct((ROWS, HD), jnp.bfloat16),
        in_specs=[vmem, vmem],
        out_specs=vmem,
        compiler_params=pltpu.CompilerParams(vmem_limit_bytes=4 * 2**20),
        name="merge",
    )(a, b)


def plane_perm(d, first):
    out = []
    for c in range(2):
        for y in range(4):
            for x in range(4):
                if (c == 0) == first:
                    to = (y, (x + d) % 4)
                else:
                    to = ((y + d) % 4, x)
                out.append(((c * 4 + y) * 4 + x, (c * 4 + to[0]) * 4 + to[1]))
    return out


def ring(n, d):
    return [(i, (i + d) % n) for i in range(n)]


def body(tokens, norm_gain, w_qkv, doc_lengths, span_start, span_len):
    z, core = lax.axis_index("z"), lax.axis_index("core")
    y, x = lax.axis_index("y"), lax.axis_index("x")
    plane = ("core", "y", "x")

    mine = jnp.concatenate([tokens, jnp.broadcast_to(norm_gain[None, :], (PAD, FEAT))], axis=0)
    side = {d: lax.ppermute(mine, plane, plane_perm(d, True)) for d in (1, -1, 2)}
    a, b = jnp.stack([mine, side[1]]), jnp.stack([side[-1], side[2]])
    far = lambda v, d: lax.ppermute(v, plane, plane_perm(d, False))
    left_a, right_b = far(a, 1), far(b, -1)
    left_b, right_a = far(b, 1), far(a, -1)
    sets = [a, b, left_a, left_b, right_a, right_b, far(left_a, 1), far(right_b, -1)]
    dk = jnp.array([k for k in STEPS for j in STEPS], jnp.int32)
    dj = jnp.array([j for k in STEPS for j in STEPS], jnp.int32)
    on_x = jnp.where(core == 0, dj, dk)
    on_y = jnp.where(core == 0, dk, dj)
    blk = ((y - on_y + 4) % 4) * 4 + (x - on_x + 4) % 4

    offs = jnp.arange(ROWS, dtype=jnp.int32)
    first_of = lambda c: (z * 2 + c) * ROWS
    lows, highs = [], []
    for c in (core, 1 - core):
        low, high = row_meta(first_of(c) + offs, doc_lengths, span_start, span_len)
        lows.append(low)
        highs.append(high)
    cosine, sine = angles(first_of(core) + offs - lows[0])
    lo, hi = jnp.stack(lows)[:, None, :], jnp.stack(highs)[:, None, :]
    slot = jnp.arange(16, dtype=jnp.int32)
    at = first_of(jnp.where(slot < 4, core, 1 - core)) + (slot % 2) * (ROWS - 1)
    low, high = row_meta(at, doc_lengths, span_start, span_len)
    meta = jnp.where(slot % 4 < 2, low, high)
    meta = jnp.where(slot == 8, z, jnp.where(slot == 9, core, meta)).astype(jnp.int32)

    w = jnp.concatenate([w_qkv[0], w_qkv[1], w_qkv[2]], axis=1)
    q, kv = project(blk, sets, w, cosine, sine)

    half = NZ // 2
    z_step = lambda v, d: lax.ppermute(v, "z", ring(NZ, d))
    put = lambda kvs, offs, state, **kw: attend(meta, q2, lo, hi, kvs, offs, state, **kw)
    up, down = z_step(kv, 1), z_step(kv, -1)
    up, q = lax.optimization_barrier((up, q))
    q2 = jnp.stack([q, lax.ppermute(q, "core", ring(2, 1))], axis=0)
    state, waiting = None, [([kv], [0])]
    for i in range(2, half + 1):
        waiting.append(([up, down], [1 - i, i - 1]))
        up = z_step(up, 1)
        if i < half:
            down = z_step(down, -1)
        for _ in range(1 if i < half else 2):
            state = put(*waiting.pop(0), state)
        up, state = lax.optimization_barrier((up, state))
    own, other = put([up], [-half], state, last_call=True)
    return merge(own, lax.ppermute(other, "core", ring(2, 1)))


def solution(mesh):
    fine = Mesh(mesh.devices.reshape(NZ, 2, 4, 4), ("z", "core", "y", "x"))
    both, plane = ("z", "core"), ("y", "x")
    return jax.shard_map(
        body,
        mesh=fine,
        in_specs=(P(both, plane), P(plane), P(None, None, plane), P(), P(), P()),
        out_specs=P(both, plane),
        check_vma=False,
    )
```
